768 devices in a mesh: doc: 96 (over z, x, core), term: 8 (over y).
Axes of the slice: x: 4, y: 8, z: 12, core: 2. Of those that a mesh axis runs over, the one named last changes fastest.
Arguments:
- tiles: bfloat16 [4608, 8, 128, 128], P('doc', 'term'), as said below
- tile_rows: int32 [4608, 8], P('doc', 'term'), may hold values from 0 to 15, as said below
- tile_cols: int32 [4608, 8], P('doc', 'term'), may hold values from 0 to 287
- tile_count: int32 [96, 8], P('doc', 'term'), may hold values from 16 to 48, as said below
- start_block: float32 [32, 196608], P(None, 'doc'), may hold values from -6 to 6
Outputs:
- next_block: float32 [32, 196608], P(None, 'doc')
The draws below stay inside these ranges and needn't reach their ends.
Inputs may be any that keep to these rules, and one draw needn't show every extreme that they name: `tile_rows`: slot s < 16 of every device names row tile s, so every row tile has a live slot on every device. `tile_count`: some device holds 48 live slots and some device 16. `tiles`: every entry is positive.
All inputs are finite; a program needn't handle non-finite values.
Results may differ from the reference program's by a relative error of at most 0.003.
Values may be sent and summed in bfloat16 or wider, within the bound.
No kernel may reach another device: no remote copies, remote signals or barrier semaphores. Data moves between devices by JAX's collectives and lax.ppermute only.
A program may use at most 64 MiB of HBM per device.

```python
import jax
import jax.numpy as jnp
from jax import lax

RT_DEV = 16
CT_DEV = 288
BLOCK = 32
TILES_DEV = 48
DOCS = 196608
N_DOC = 96
N_TERM = 8


def draw_tiles(key, part):
    key = jax.random.fold_in(key, 4)
    first, second = jax.random.split(key, 2)
    shape = (N_DOC * TILES_DEV, N_TERM, 128, 128)
    base = jax.random.uniform(first, shape, jnp.float32, 0.05, 1.0)
    column = jnp.exp(jax.random.uniform(second, (N_DOC * TILES_DEV, N_TERM, 1, 128), jnp.float32, 0.0, 2.0))
    values = base * base * column
    return values.astype(jnp.bfloat16)


def draw_tile_rows(key, part):
    key = jax.random.fold_in(key, 1)
    shape = (N_DOC * TILES_DEV, N_TERM)
    slot = jax.lax.broadcasted_iota(jnp.int32, shape, 0) % TILES_DEV
    drawn = jax.random.randint(key, shape, 0, RT_DEV, dtype=jnp.int32)
    return jnp.where(slot < RT_DEV, slot, drawn)


def draw_tile_cols(key, part):
    key = jax.random.fold_in(key, 2)
    return jax.random.randint(key, (N_DOC * TILES_DEV, N_TERM), 0, CT_DEV, dtype=jnp.int32)


def draw_tile_count(key, part):
    key = jax.random.fold_in(key, 3)
    first, second, third = jax.random.split(key, 3)
    total = N_DOC * N_TERM
    counts = jax.random.randint(first, (total,), RT_DEV, TILES_DEV + 1, dtype=jnp.int32)
    fullest = jax.random.randint(second, (), 0, total, dtype=jnp.int32)
    emptiest = (fullest + 1 + jax.random.randint(third, (), 0, total - 1, dtype=jnp.int32)) % total
    places = jnp.arange(total, dtype=jnp.int32)
    counts = jnp.where(places == fullest, TILES_DEV, counts)
    counts = jnp.where(places == emptiest, RT_DEV, counts)
    return counts.reshape(N_DOC, N_TERM)


def shard_levels(rng, shape, cuts, smallest, largest):
    level, own = 1.0, jax.random.fold_in(rng, 6)
    for axis_at, blocks in cuts:
        steps = jnp.exp(jax.random.uniform(jax.random.fold_in(own, axis_at), (blocks,), jnp.float32, smallest / len(cuts), largest / len(cuts)))
        level = level * jnp.repeat(steps, shape[axis_at] // blocks).reshape([-1 if axis == axis_at else 1 for axis in range(len(shape))])
    return level


def bell_draw(rng, extent, scale, limit, cuts=(), kind=jnp.bfloat16):
    loudness = shard_levels(rng, extent, cuts, -0.22, 0.18) if cuts else 1.0
    array = jax.random.normal(rng, extent, jnp.float32) * scale * loudness
    return jnp.minimum(jnp.maximum(array, -limit), limit).astype(kind)


def setup_inputs(seed: int = 0) -> dict:
    splits = jax.random.split(jax.random.key(seed), 6)
    return {
        "tiles": draw_tiles(jax.random.fold_in(splits[5], 71), 0),
        "tile_rows": draw_tile_rows(jax.random.fold_in(splits[5], 71), 0),
        "tile_cols": draw_tile_cols(jax.random.fold_in(splits[5], 71), 0),
        "tile_count": draw_tile_count(jax.random.fold_in(splits[5], 71), 0),
        "start_block": bell_draw(splits[4], (BLOCK, DOCS), 1.0, 6.0, ((1, 96),), jnp.float32),
    }


highest = lax.Precision.HIGHEST

def device_view(tiles, tile_rows, tile_cols, tile_count):
    tiles_dev = tiles.reshape(N_DOC, TILES_DEV, N_TERM, 128, 128)
    rows_dev = tile_rows.reshape(N_DOC, TILES_DEV, N_TERM)
    offsets = (jnp.arange(N_TERM, dtype=jnp.int32) * CT_DEV)[None, None, :]
    cols_dev = tile_cols.reshape(N_DOC, TILES_DEV, N_TERM) + offsets
    slots = jnp.arange(TILES_DEV, dtype=jnp.int32)[None, :, None]
    live = (slots < tile_count[:, None, :]).astype(jnp.float32)
    return (tiles_dev, rows_dev, cols_dev, live)

def row_squares(tiles_dev, rows_dev, live):

    def one_block(args):
        tile_block, rows, alive = args
        sums = lax.optimization_barrier(jnp.sum(jnp.square(tile_block.astype(jnp.float32)), axis=3)) * alive[:, :, None]
        return jax.ops.segment_sum(sums.reshape(-1, 128), rows.reshape(-1), num_segments=RT_DEV)
    return lax.map(one_block, (tiles_dev, rows_dev, live)).reshape(-1)

def term_side(vectors, tiles_dev, rows_dev, cols_dev, live):
    width = vectors.shape[0]
    blocks = vectors.reshape(width, N_DOC, RT_DEV, 128).transpose(1, 0, 2, 3)

    def one_block(total, args):
        block, tile_block, rows, cols, alive = args
        picked = block[:, rows, :].astype(jnp.float32)
        terms = jnp.einsum('wtnk,tnkc->tnwc', picked, tile_block.astype(jnp.float32), precision=highest)
        terms = terms * alive[:, :, None, None]
        total = total + jax.ops.segment_sum(terms.reshape(-1, width, 128), cols.reshape(-1), num_segments=N_TERM * CT_DEV)
        return (total, None)
    start = jnp.zeros((N_TERM * CT_DEV, width, 128), jnp.float32)
    total, _ = lax.scan(one_block, start, (blocks, tiles_dev, rows_dev, cols_dev, live))
    return total.transpose(1, 0, 2).reshape(width, -1)

def doc_side(vectors, tiles_dev, rows_dev, cols_dev, live):
    width = vectors.shape[0]
    table = vectors.reshape(width, N_TERM * CT_DEV, 128)

    def one_block(args):
        tile_block, rows, cols, alive = args
        picked = table[:, cols, :].astype(jnp.float32)
        terms = jnp.einsum('wtnj,tnkj->tnwk', picked, tile_block.astype(jnp.float32), precision=highest)
        terms = terms * alive[:, :, None, None]
        return jax.ops.segment_sum(terms.reshape(-1, width, 128), rows.reshape(-1), num_segments=RT_DEV)
    parts = lax.map(one_block, (tiles_dev, rows_dev, cols_dev, live))
    return parts.transpose(2, 0, 1, 3).reshape(width, -1)

def reference(tiles, tile_rows, tile_cols, tile_count, start_block):
    tiles_dev, rows_dev, cols_dev, live = device_view(tiles, tile_rows, tile_cols, tile_count)
    inverse_norm = 1.0 / jnp.sqrt(row_squares(tiles_dev, rows_dev, live))
    weights = inverse_norm.astype(jnp.bfloat16)[None, :]
    column_mass = term_side(weights, tiles_dev, rows_dev, cols_dev, live).astype(jnp.bfloat16)
    degree = inverse_norm * doc_side(column_mass, tiles_dev, rows_dev, cols_dev, live)[0]
    scale = inverse_norm / jnp.sqrt(degree)

    def apply(block):
        scaled = (block * scale[None, :]).astype(jnp.bfloat16)
        summed = term_side(scaled, tiles_dev, rows_dev, cols_dev, live).astype(jnp.bfloat16)
        return doc_side(summed, tiles_dev, rows_dev, cols_dev, live) * scale[None, :]

    def gram(left, right):
        return jnp.dot(left, right.T, precision=highest) / DOCS

    def normalize(block):
        factor = jnp.linalg.cholesky(gram(block, block))
        return (factor, jax.scipy.linalg.solve_triangular(factor, block, lower=True))
    factor0, basis0 = normalize(start_block)
    image0 = apply(basis0)
    coeff0 = gram(image0, basis0)
    residual0 = image0 - jnp.dot(coeff0, basis0, precision=highest)
    factor1, next_block = normalize(residual0)
    return next_block
```

```python
import jax
import jax.numpy as jnp
from jax import lax
from jax.experimental import pallas as pl
from jax.experimental.pallas import tpu as pltpu
from jax.sharding import Mesh, PartitionSpec as P

CT_DEV = 288
RT_DEV = 16
BLOCK = 32
SLOTS = 48
SIDE = 128
NZ, NX, NC, NY = 12, 4, 2, 8
NXC = NX * NC
PER_XC = CT_DEV // NXC
PER_Z = PER_XC // NZ
GROUP = 8
DOCS = RT_DEV * SIDE * NZ * NXC

F32 = jnp.float32
B16 = jnp.bfloat16
highest = lax.Precision.HIGHEST

VMEM = pl.BlockSpec(memory_space=pltpu.VMEM)
SMEM = pl.BlockSpec(memory_space=pltpu.SMEM)


def dot_nn(a, b, **kw):
    return lax.dot_general(a, b, (((1,), (0,)), ((), ())), preferred_element_type=F32, **kw)


def dot_nt(a, b, **kw):
    return lax.dot_general(a, b, (((1,), (1,)), ((), ())), preferred_element_type=F32, **kw)


def over_slots(count, step):
    def group(g, carry):
        for i in range(GROUP):
            s = g * GROUP + i
            step(s, s < count)
        return carry

    lax.fori_loop(0, (count + GROUP - 1) // GROUP, group, 0)


def inverse_factor(matrix):
    n = matrix.shape[0]
    at_row = lax.broadcasted_iota(jnp.int32, (n, n), 0)
    at_col = lax.broadcasted_iota(jnp.int32, (n, n), 1)
    eye = (at_row == at_col).astype(F32)
    work = jnp.concatenate([matrix, eye], axis=1)
    row_id = lax.broadcasted_iota(jnp.int32, (n, 1), 0)
    for j in range(n):
        ratio = jnp.where(row_id > j, work[:, j : j + 1] / work[j : j + 1, j : j + 1], 0.0)
        work = work - ratio * work[j : j + 1, :]
    diag = jnp.sum(work[:, :n] * eye, axis=1, keepdims=True)
    return work[:, n:] / jnp.sqrt(diag)


def squares_kernel(count, rows, tiles, start, copies, gram, total):
    total[...] = jnp.zeros_like(total)
    ones = jnp.ones((8, SIDE), B16)

    def step(s, live):
        tile = tiles[s].astype(F32)
        sq = tile * tile
        high = sq.astype(B16)
        low = (sq - high.astype(F32)).astype(B16)
        part = dot_nt(ones, high) + dot_nt(ones, low)
        total[pl.ds(rows[s], 1), :] += jnp.where(live, part[0:1], 0.0)

    over_slots(count[0], step)
    for k in range(NY):
        copies[k] = total[...]
    v = start[...]
    gram[...] = jnp.concatenate(
        [dot_nt(v, v, precision=highest), jnp.zeros((BLOCK, SIDE - BLOCK), F32)], axis=1
    )


def mass_kernel(count, rows, cols, tiles, squares, gram, inverse_norm, out, weights):
    inv = 1.0 / jnp.sqrt(jnp.sum(squares[...], axis=0))
    inverse_norm[...] = inv
    weights[...] = inv.astype(B16).astype(F32)
    out[...] = jnp.zeros_like(out)

    def step(s, live):
        w = jnp.broadcast_to(weights[pl.ds(rows[s], 1), :], (8, SIDE)).astype(B16)
        part = dot_nn(w, tiles[s])
        col = cols[s]
        owner = col // PER_XC
        out[owner, pl.ds(col - owner * PER_XC, 1), :] += jnp.where(live, part[0:1], 0.0)

    over_slots(count[0], step)
    for k in range(NXC):
        out[k, PER_XC : PER_XC + 4] = gram[4 * k : 4 * k + 4]


def split_three(value):
    high = value.astype(B16)
    rest = value - high.astype(F32)
    middle = rest.astype(B16)
    return [high, middle, (rest - middle.astype(F32)).astype(B16)]


def mass_partial_kernel(parts, out):
    total = jnp.sum(parts[...], axis=0)
    gram = jnp.concatenate([total[PER_XC:], jnp.zeros((4, SIDE), F32)], axis=0)
    packed = jnp.concatenate([part.astype(F32)[0:4] for part in split_three(gram)], axis=0)
    packed = jnp.concatenate([total[0:PER_XC], packed], axis=0).astype(B16)
    for j in range(NZ):
        out[j] = packed


def mass_total_kernel(parts, out):
    total = jnp.sum(parts[...].astype(F32), axis=0)
    gram = total[PER_XC : PER_XC + 4] + total[PER_XC + 4 : PER_XC + 8] + total[PER_XC + 8 :]
    gram = jnp.concatenate([gram, jnp.zeros((4, SIDE), F32)], axis=0)
    packed = jnp.concatenate([part.astype(F32)[0:4] for part in split_three(gram)], axis=0)
    packed = jnp.concatenate([total[0:PER_XC], packed], axis=0).astype(B16)
    for k in range(NXC):
        out[k] = packed


def degree_kernel(count, rows, cols, tiles, packed, start, copies, basis, total, mass):
    total[...] = jnp.zeros_like(total)
    for k in range(NXC):
        mass[k] = packed[k].astype(F32)

    def step(s, live):
        col = cols[s]
        owner = col // PER_XC
        m = mass[owner, pl.ds(col - owner * PER_XC, 1), :]
        part = dot_nt(jnp.broadcast_to(m, (8, SIDE)).astype(B16), tiles[s])
        total[pl.ds(rows[s], 1), :] += jnp.where(live, part[0:1], 0.0)

    over_slots(count[0], step)
    for k in range(NY):
        copies[k] = total[...]
    thirds = [
        jnp.concatenate(
            [mass[k, PER_XC + 4 * i : PER_XC + 4 * i + 4, 0:BLOCK] for k in range(NXC)], axis=0
        )
        for i in range(3)
    ]
    gram = thirds[0] + thirds[1] + thirds[2]
    inverse = inverse_factor(gram * (1.0 / DOCS))
    whole = dot_nn(inverse, start[...], precision=highest)
    for r in range(RT_DEV):
        basis[r] = whole[:, r * SIDE : (r + 1) * SIDE]


def term_kernel(count, rows, cols, tiles, degrees, inverse_norm, basis, scale, out, scaled, total):
    inv = inverse_norm[...]
    degree = inv * jnp.sum(degrees[...], axis=0)
    s_all = inv / jnp.sqrt(degree)
    scale[...] = s_all
    for r in range(RT_DEV):
        scaled[r] = (basis[r] * s_all[r : r + 1, :]).astype(B16)

    def clear(i, carry):
        total[pl.ds(i * 8, 8)] = jnp.zeros((8, BLOCK, SIDE), F32)
        return carry

    lax.fori_loop(0, CT_DEV // 8, clear, 0)

    def step(s, live):
        part = dot_nn(scaled[rows[s]], tiles[s])
        total[cols[s]] += jnp.where(live, part, 0.0)

    over_slots(count[0], step)

    def write(i, carry):
        out[pl.ds(i * 8, 8)] = total[pl.ds(i * 8, 8)].astype(B16)
        return carry

    lax.fori_loop(0, CT_DEV // 8, write, 0)


def doc_kernel(count, rows, cols, tiles, table, out):
    out[...] = jnp.zeros_like(out)

    def step(s, live):
        part = dot_nt(table[cols[s]], tiles[s])
        out[rows[s]] += jnp.where(live, part, 0.0)

    over_slots(count[0], step)


def image_kernel(summed, scale, basis, image, copies, both):
    for r in range(RT_DEV):
        block = summed[r] * scale[r : r + 1, :]
        image[r] = block
        both[0:BLOCK, r * SIDE : (r + 1) * SIDE] = block
        both[BLOCK : 2 * BLOCK, r * SIDE : (r + 1) * SIDE] = basis[r]
    grams = dot_nt(both[0:BLOCK, :], both[...], precision=highest)
    packed = jnp.concatenate([grams[0:16], grams[16:32]], axis=1)
    for k in range(NXC):
        copies[k] = packed


def gram_kernel(parts, copies):
    total = jnp.sum(parts[...], axis=0)
    for j in range(NZ):
        copies[j] = total


def last_kernel(parts, image, basis, out, both):
    total = jnp.sum(parts[...], axis=0) * (1.0 / DOCS)
    grams = jnp.concatenate([total[:, 0 : 2 * BLOCK], total[:, 2 * BLOCK :]], axis=0)
    coeff = grams[:, BLOCK:]
    inverse = inverse_factor(grams[:, 0:BLOCK] - dot_nt(coeff, coeff, precision=highest))
    for r in range(RT_DEV):
        both[0:BLOCK, r * SIDE : (r + 1) * SIDE] = image[r]
        both[BLOCK : 2 * BLOCK, r * SIDE : (r + 1) * SIDE] = basis[r]
    mix = jnp.concatenate([inverse, -dot_nn(inverse, coeff, precision=highest)], axis=1)
    out[...] = dot_nn(mix, both[...], precision=highest)


def call(kernel, ins, outs, scratch=(), scalars=0):
    shapes = [jax.ShapeDtypeStruct(shape, kind) for shape, kind in outs]
    return pl.pallas_call(
        kernel,
        out_shape=shapes,
        in_specs=[SMEM] * scalars + [VMEM] * (len(ins) - scalars),
        out_specs=[VMEM] * len(shapes),
        scratch_shapes=[pltpu.VMEM(shape, kind) for shape, kind in scratch],
        compiler_params=pltpu.CompilerParams(vmem_limit_bytes=32 * 1024 * 1024),
        name=kernel.__name__,
    )(*ins)


def swap(value, axes):
    return lax.all_to_all(value, axes, 0, 0, tiled=True)


XC = ("x", "core")


def body(tiles, tile_rows, tile_cols, tile_count, start):
    tiles = tiles.reshape(SLOTS, SIDE, SIDE)
    rows = tile_rows.reshape(SLOTS)
    cols = tile_cols.reshape(SLOTS)
    count = tile_count.reshape(1)
    full = (RT_DEV, SIDE)
    wide = (RT_DEV, BLOCK, SIDE)

    squares, gram = call(
        squares_kernel,
        (count, rows, tiles, start),
        [((NY, *full), F32), ((BLOCK, SIDE), F32)],
        [(full, F32)],
        scalars=2,
    )
    squares = swap(squares, "term")
    inverse_norm, mass = call(
        mass_kernel,
        (count, rows, cols, tiles, squares, gram),
        [(full, F32), ((NXC, PER_XC + 4, SIDE), F32)],
        [(full, F32)],
        scalars=3,
    )
    (mass,) = call(mass_partial_kernel, (swap(mass, XC),), [((NZ, PER_XC + 12, SIDE), B16)])
    (mass,) = call(mass_total_kernel, (swap(mass, "z"),), [((NXC, PER_XC + 12, SIDE), B16)])
    mass = swap(mass, XC)
    degrees, basis = call(
        degree_kernel,
        (count, rows, cols, tiles, mass, start),
        [((NY, *full), F32), (wide, F32)],
        [(full, F32), ((NXC, PER_XC + 12, SIDE), F32)],
        scalars=3,
    )
    degrees = swap(degrees, "term")
    scale, terms = call(
        term_kernel,
        (count, rows, cols, tiles, degrees, inverse_norm, basis),
        [(full, F32), ((CT_DEV, BLOCK, SIDE), B16)],
        [(wide, B16), ((CT_DEV, BLOCK, SIDE), F32)],
        scalars=3,
    )

    def reduce(value, axes, parts):
        moved = swap(value, axes)
        moved = moved.reshape(parts, value.shape[0] // parts, BLOCK, SIDE)
        return jnp.sum(moved.astype(F32), axis=0)

    def spread(value, axes, parts):
        return swap(jnp.tile(value, (parts, 1, 1)), axes)

    terms = reduce(terms, "core", NC).astype(B16)
    terms = reduce(terms, "x", NX).astype(B16)
    terms = reduce(terms, "z", NZ).astype(B16)
    terms = spread(terms, "z", NZ)
    terms = spread(terms, "x", NX)
    terms = spread(terms, "core", NC)
    (partial,) = call(doc_kernel, (count, rows, cols, tiles, terms), [(wide, F32)], scalars=3)
    summed = spread(reduce(partial, "term", NY), "term", NY)
    image, grams = call(
        image_kernel,
        (summed, scale, basis),
        [(wide, F32), ((NXC, 16, SIDE), F32)],
        [((2 * BLOCK, RT_DEV * SIDE), F32)],
    )
    (grams,) = call(gram_kernel, (swap(grams, XC),), [((NZ, 16, SIDE), F32)])
    (next_block,) = call(
        last_kernel,
        (swap(grams, "z"), image, basis),
        [((BLOCK, RT_DEV * SIDE), F32)],
        [((2 * BLOCK, RT_DEV * SIDE), F32)],
    )
    return next_block


def solution(mesh):
    doc = ("z", "x", "core")
    fine = Mesh(mesh.devices.reshape(NZ, NX, NC, NY), (*doc, "term"))
    in_specs = (
        P(doc, "term", None, None),
        P(doc, "term"),
        P(doc, "term"),
        P(doc, "term"),
        P(None, doc),
    )
    return jax.shard_map(body, mesh=fine, in_specs=in_specs, out_specs=P(None, doc), check_vma=False)
```

```python
import jax
import jax.numpy as jnp
from jax import lax
from jax.experimental import pallas as pl
from jax.experimental.pallas import tpu as pltpu
from jax.sharding import Mesh, PartitionSpec as P

CT_DEV = 288
RT_DEV = 16
BLOCK = 32
SLOTS = 48
SIDE = 128
NZ, NX, NC, NY = 12, 4, 2, 8
NPAIR = 2
NFAR = NZ // NPAIR
NEAR = NPAIR * NX
NXC = NX * NC
PER_XC = CT_DEV // NXC
PER_Z = PER_XC // NZ
PER_NEAR = CT_DEV // NC // NEAR
GROUP = 8
ROW = 2
COL = ROW + SLOTS
PANEL = 8
HALF = CT_DEV // NC
DOCS = RT_DEV * SIDE * NZ * NXC

F32 = jnp.float32
B16 = jnp.bfloat16
SENT = B16
highest = lax.Precision.HIGHEST

VMEM = pl.BlockSpec(memory_space=pltpu.VMEM)
SMEM = pl.BlockSpec(memory_space=pltpu.SMEM)


def dot_nn(a, b, **kw):
    return lax.dot_general(a, b, (((1,), (0,)), ((), ())), preferred_element_type=F32, **kw)


def dot_nt(a, b, **kw):
    return lax.dot_general(a, b, (((1,), (1,)), ((), ())), preferred_element_type=F32, **kw)


def over_slots(count, step):
    def group(g, carry):
        for i in range(GROUP):
            s = g * GROUP + i
            step(s, s < count)
        return carry

    lax.fori_loop(0, (count + GROUP - 1) // GROUP, group, 0)


def inverse_factor(matrix):
    n = matrix.shape[0]
    width = 2 * n
    at_row = lax.broadcasted_iota(jnp.int32, (n, n), 0)
    at_col = lax.broadcasted_iota(jnp.int32, (n, n), 1)
    eye = (at_row == at_col).astype(F32)
    work = jnp.concatenate([matrix, eye], axis=1)
    row_id = lax.broadcasted_iota(jnp.int32, (n, width), 0)
    for first in range(0, n, PANEL):
        columns = [
            jnp.broadcast_to(work[:, first + k : first + k + 1], (n, width)) for k in range(PANEL)
        ]
        for k in range(PANEL):
            j = first + k
            ratio = jnp.where(row_id > j, columns[k] * (1.0 / columns[k][j : j + 1]), 0.0)
            for m in range(k + 1, PANEL):
                columns[m] = columns[m] - ratio * columns[m][j : j + 1]
            work = work - ratio * work[j : j + 1]
    diag = jnp.sum(work[:, :n] * eye, axis=1, keepdims=True)
    return work[:, n:] / jnp.sqrt(diag)


def squares_kernel(ints, tiles, copies, held, total, sems):
    def copy(g):
        at = pl.ds(g * GROUP, GROUP)
        return pltpu.make_async_copy(tiles.at[at], held.at[at], sems.at[g])

    for g in range(SLOTS // GROUP):
        copy(g).start()
    total[...] = jnp.zeros_like(total)
    ones = jnp.ones((8, SIDE), B16)
    for g in range(SLOTS // GROUP):
        copy(g).wait()

        @pl.when(g * GROUP < ints[0])
        def _():
            for i in range(GROUP):
                s = g * GROUP + i
                tile = held[s].astype(F32)
                sq = tile * tile
                high = sq.astype(B16)
                low = (sq - high.astype(F32)).astype(B16)
                part = dot_nt(ones, high) + dot_nt(ones, low)
                total[pl.ds(ints[ROW + s], 1), :] += jnp.where(s < ints[0], part[0:1], 0.0)

    for k in range(NY):
        copies[k] = total[...]


def mass_kernel(ints, tiles, squares, start, inverse_norm, out, weights):
    inv = 1.0 / jnp.sqrt(jnp.sum(squares[...], axis=0))
    inverse_norm[...] = inv
    weights[...] = inv.astype(B16).astype(F32)
    out[...] = jnp.zeros_like(out)

    def step(s, live):
        w = jnp.broadcast_to(weights[pl.ds(ints[ROW + s], 1), :], (8, SIDE)).astype(B16)
        part = dot_nn(w, tiles[s])
        col = ints[COL + s]
        owner = col // PER_XC
        out[owner, pl.ds(col - owner * PER_XC, 1), :] += jnp.where(live, part[0:1], 0.0)

    over_slots(ints[0], step)
    v = start[...]
    gram = jnp.concatenate(
        [dot_nt(v, v, precision=highest), jnp.zeros((BLOCK, SIDE - BLOCK), F32)], axis=1
    )
    for k in range(NXC):
        out[k, PER_XC : PER_XC + 4] = gram[4 * k : 4 * k + 4]


def split_three(value):
    high = value.astype(B16)
    rest = value - high.astype(F32)
    middle = rest.astype(B16)
    return [high, middle, (rest - middle.astype(F32)).astype(B16)]


def mass_partial_kernel(parts, out):
    total = jnp.sum(parts[...], axis=0)
    gram = jnp.concatenate([total[PER_XC:], jnp.zeros((4, SIDE), F32)], axis=0)
    packed = jnp.concatenate([part.astype(F32)[0:4] for part in split_three(gram)], axis=0)
    packed = jnp.concatenate([total[0:PER_XC], packed], axis=0).astype(B16)
    for j in range(NZ):
        out[j] = packed


def mass_total_kernel(parts, out):
    total = jnp.sum(parts[...].astype(F32), axis=0)
    gram = total[PER_XC : PER_XC + 4] + total[PER_XC + 4 : PER_XC + 8] + total[PER_XC + 8 :]
    gram = jnp.concatenate([gram, jnp.zeros((4, SIDE), F32)], axis=0)
    packed = jnp.concatenate([part.astype(F32)[0:4] for part in split_three(gram)], axis=0)
    packed = jnp.concatenate([total[0:PER_XC], packed], axis=0).astype(B16)
    for k in range(NXC):
        out[k] = packed


def degree_kernel(ints, tiles, packed, start, copies, basis, total, mass):
    total[...] = jnp.zeros_like(total)
    for k in range(NXC):
        mass[k] = packed[k].astype(F32)

    def step(s, live):
        col = ints[COL + s]
        owner = col // PER_XC
        m = mass[owner, pl.ds(col - owner * PER_XC, 1), :]
        part = dot_nt(jnp.broadcast_to(m, (8, SIDE)).astype(B16), tiles[s])
        total[pl.ds(ints[ROW + s], 1), :] += jnp.where(live, part[0:1], 0.0)

    over_slots(ints[0], step)
    for k in range(NY):
        copies[k] = total[...]
    thirds = [
        jnp.concatenate(
            [mass[k, PER_XC + 4 * i : PER_XC + 4 * i + 4, 0:BLOCK] for k in range(NXC)], axis=0
        )
        for i in range(3)
    ]
    gram = thirds[0] + thirds[1] + thirds[2]
    inverse = inverse_factor(gram * (1.0 / DOCS))
    whole = dot_nn(inverse, start[...], precision=highest)
    for r in range(RT_DEV):
        basis[r] = whole[:, r * SIDE : (r + 1) * SIDE]


def term_kernel(
    ints, tiles, degrees, inverse_norm, basis, scale, keep, send, scaled, total
):
    inv = inverse_norm[...]
    degree = inv * jnp.sum(degrees[...], axis=0)
    s_all = inv / jnp.sqrt(degree)
    scale[...] = s_all
    for r in range(RT_DEV):
        scaled[r] = (basis[r] * s_all[r : r + 1, :]).astype(B16)

    def clear(i, carry):
        total[pl.ds(i * 8, 8)] = jnp.zeros((8, BLOCK, SIDE), F32)
        return carry

    lax.fori_loop(0, CT_DEV // 8, clear, 0)

    def step(s, live):
        part = dot_nn(scaled[ints[ROW + s]], tiles[s])
        total[ints[COL + s]] += jnp.where(live, part, 0.0)

    over_slots(ints[0], step)
    mine = ints[1] * HALF
    other = HALF - mine

    def write(i, carry):
        keep[pl.ds(i * 8, 8)] = total[pl.ds(mine + i * 8, 8)].astype(B16)
        send[pl.ds(i * 8, 8)] = total[pl.ds(other + i * 8, 8)].astype(B16)
        return carry

    lax.fori_loop(0, HALF // 8, write, 0)


def pair_kernel(left, right, out):
    def step(i, carry):
        at = pl.ds(i * 8, 8)
        out[at] = (left[at].astype(F32) + right[at].astype(F32)).astype(B16)
        return carry

    lax.fori_loop(0, HALF // 8, step, 0)


def close_sum_kernel(parts, out):
    def step(i, carry):
        at = pl.ds(i * PER_Z, PER_Z)
        total = parts[0, at].astype(F32)
        for k in range(1, NEAR):
            total += parts[k, at].astype(F32)
        out[at] = total.astype(B16)
        return carry

    lax.fori_loop(0, PER_NEAR // PER_Z, step, 0)


def far_sum_kernel(parts, out):
    total = parts[0].astype(F32)
    for k in range(1, NFAR):
        total += parts[k].astype(F32)
    total = total.astype(B16)
    for k in range(NFAR):
        out[k] = total


def image_sum_kernel(parts, out):
    total = parts[0].astype(F32)
    for k in range(1, NY):
        total += parts[k].astype(F32)
    for k in range(NY):
        out[k] = total


def doc_kernel(ints, tiles, own, other, out, total):
    total[...] = jnp.zeros_like(total)
    mine = ints[1]

    def step(s, live):
        col = ints[COL + s]
        half = (col >= HALF).astype(jnp.int32)
        at = col - half * HALF
        part = dot_nt(jnp.where(half == mine, own[at], other[at]), tiles[s])
        total[ints[ROW + s]] += jnp.where(live, part, 0.0)

    over_slots(ints[0], step)
    for r in range(RT_DEV):
        out[r] = total[r].astype(out.dtype)


def image_kernel(summed, scale, basis, image, copies, both):
    for r in range(RT_DEV):
        block = summed[r] * scale[r : r + 1, :]
        image[r] = block
        both[0:BLOCK, r * SIDE : (r + 1) * SIDE] = block
        both[BLOCK : 2 * BLOCK, r * SIDE : (r + 1) * SIDE] = basis[r]
    grams = dot_nt(both[0:BLOCK, :], both[...], precision=highest)
    packed = jnp.concatenate([grams[0:16], grams[16:32]], axis=1)
    for k in range(NXC):
        copies[k] = packed


def gram_kernel(parts, copies):
    total = jnp.sum(parts[...], axis=0)
    for j in range(NZ):
        copies[j] = total


def last_kernel(parts, image, basis, out, both):
    total = jnp.sum(parts[...], axis=0) * (1.0 / DOCS)
    grams = jnp.concatenate([total[:, 0 : 2 * BLOCK], total[:, 2 * BLOCK :]], axis=0)
    coeff = grams[:, BLOCK:]
    inverse = inverse_factor(grams[:, 0:BLOCK] - dot_nt(coeff, coeff, precision=highest))
    for r in range(RT_DEV):
        both[0:BLOCK, r * SIDE : (r + 1) * SIDE] = image[r]
        both[BLOCK : 2 * BLOCK, r * SIDE : (r + 1) * SIDE] = basis[r]
    mix = jnp.concatenate([inverse, -dot_nn(inverse, coeff, precision=highest)], axis=1)
    out[...] = dot_nn(mix, both[...], precision=highest)


def call(kernel, ins, outs, scratch=(), scalars=0, specs=None):
    shapes = [jax.ShapeDtypeStruct(shape, kind) for shape, kind in outs]
    return pl.pallas_call(
        kernel,
        out_shape=shapes,
        in_specs=specs or [SMEM] * scalars + [VMEM] * (len(ins) - scalars),
        out_specs=[VMEM] * len(shapes),
        scratch_shapes=[s if not isinstance(s, tuple) else pltpu.VMEM(*s) for s in scratch],
        compiler_params=pltpu.CompilerParams(vmem_limit_bytes=20 * 1024 * 1024),
        name=kernel.__name__,
    )(*ins)


def swap(value, axes):
    return lax.all_to_all(value, axes, 0, 0, tiled=True)


XC = ("x", "core")
Z = ("far", "pair")
CLOSE = ("pair", "x")


def body(tiles, tile_rows, tile_cols, tile_count, start):
    tiles = tiles.reshape(SLOTS, SIDE, SIDE)
    ints = jnp.concatenate(
        [
            tile_count.reshape(1),
            lax.axis_index("core").reshape(1),
            tile_rows.reshape(SLOTS),
            tile_cols.reshape(SLOTS),
        ]
    )
    full = (RT_DEV, SIDE)
    wide = (RT_DEV, BLOCK, SIDE)

    (squares,) = call(
        squares_kernel,
        (ints, tiles),
        [((NY, *full), F32)],
        [
            pltpu.VMEM((SLOTS, SIDE, SIDE), B16),
            pltpu.VMEM(full, F32),
            pltpu.SemaphoreType.DMA((SLOTS // GROUP,)),
        ],
        specs=[SMEM, pl.BlockSpec(memory_space=pltpu.HBM)],
    )
    squares = swap(squares, "term")
    inverse_norm, mass = call(
        mass_kernel,
        (ints, tiles, squares, start),
        [(full, F32), ((NXC, PER_XC + 4, SIDE), F32)],
        [(full, F32)],
        scalars=1,
    )
    (mass,) = call(mass_partial_kernel, (swap(mass, XC),), [((NZ, PER_XC + 12, SIDE), B16)])
    (mass,) = call(mass_total_kernel, (swap(mass, Z),), [((NXC, PER_XC + 12, SIDE), B16)])
    mass = swap(mass, XC)
    degrees, basis = call(
        degree_kernel,
        (ints, tiles, mass, start),
        [((NY, *full), F32), (wide, F32)],
        [(full, F32), ((NXC, PER_XC + 12, SIDE), F32)],
        scalars=1,
    )
    degrees = swap(degrees, "term")
    half = (HALF, BLOCK, SIDE)
    scale, keep, send = call(
        term_kernel,
        (ints, tiles, degrees, inverse_norm, basis),
        [(full, F32), (half, B16), (half, B16)],
        [(wide, B16), ((CT_DEV, BLOCK, SIDE), F32)],
        scalars=1,
    )

    def other_core(value):
        return lax.ppermute(value, "core", [(0, 1), (1, 0)])

    def spread(value, axes, parts):
        return swap(jnp.tile(value, (parts, 1, 1)), axes)

    (terms,) = call(pair_kernel, (keep, other_core(send)), [(half, B16)])
    terms = swap(terms, CLOSE).reshape(NEAR, PER_NEAR, BLOCK, SIDE)
    (terms,) = call(close_sum_kernel, (terms,), [((PER_NEAR, BLOCK, SIDE), B16)])
    terms = swap(terms, "far").reshape(NFAR, PER_Z, BLOCK, SIDE)
    (terms,) = call(far_sum_kernel, (terms,), [((NFAR, PER_Z, BLOCK, SIDE), B16)])
    terms = swap(terms.reshape(PER_NEAR, BLOCK, SIDE), "far")
    terms = spread(terms, CLOSE, NEAR)
    (partial,) = call(
        doc_kernel,
        (ints, tiles, terms, other_core(terms)),
        [(wide, SENT)],
        [(wide, F32)],
        scalars=1,
    )
    partial = swap(partial, "term").reshape(NY, RT_DEV // NY, BLOCK, SIDE)
    (summed,) = call(image_sum_kernel, (partial,), [((NY, RT_DEV // NY, BLOCK, SIDE), F32)])
    summed = swap(summed.reshape(wide), "term")
    image, grams = call(
        image_kernel,
        (summed, scale, basis),
        [(wide, F32), ((NXC, 16, SIDE), F32)],
        [((2 * BLOCK, RT_DEV * SIDE), F32)],
    )
    (grams,) = call(gram_kernel, (swap(grams, XC),), [((NZ, 16, SIDE), F32)])
    (next_block,) = call(
        last_kernel,
        (swap(grams, Z), image, basis),
        [((BLOCK, RT_DEV * SIDE), F32)],
        [((2 * BLOCK, RT_DEV * SIDE), F32)],
    )
    return next_block


def solution(mesh):
    doc = ("far", "pair", "x", "core")
    fine = Mesh(mesh.devices.reshape(NFAR, NPAIR, NX, NC, NY), (*doc, "term"))
    in_specs = (
        P(doc, "term", None, None),
        P(doc, "term"),
        P(doc, "term"),
        P(doc, "term"),
        P(None, doc),
    )
    return jax.shard_map(body, mesh=fine, in_specs=in_specs, out_specs=P(None, doc), check_vma=False)
```

```python
import jax
import jax.numpy as jnp
from jax import lax
from jax.experimental import pallas as pl
from jax.experimental.pallas import tpu as pltpu
from jax.sharding import Mesh, PartitionSpec as P

CT_DEV = 288
RT_DEV = 16
BLOCK = 32
SLOTS = 48
SIDE = 128
NZ, NX, NC, NY = 12, 4, 2, 8
NPAIR = 2
NFAR = NZ // NPAIR
NEAR = NPAIR * NX
NXC = NX * NC
PER_XC = CT_DEV // NXC
PER_Z = PER_XC // NZ
PER_NEAR = CT_DEV // NC // NEAR
ROW = 2
COL = ROW + SLOTS
PANEL = 16
HALF = CT_DEV // NC
DOCS = RT_DEV * SIDE * NZ * NXC

F32 = jnp.float32
B16 = jnp.bfloat16
SENT = B16
highest = lax.Precision.HIGHEST

VMEM = pl.BlockSpec(memory_space=pltpu.VMEM)
SMEM = pl.BlockSpec(memory_space=pltpu.SMEM)


def dot_nn(a, b, **kw):
    return lax.dot_general(a, b, (((1,), (0,)), ((), ())), preferred_element_type=F32, **kw)


def dot_nt(a, b, **kw):
    return lax.dot_general(a, b, (((1,), (1,)), ((), ())), preferred_element_type=F32, **kw)


def over_slots(count, step):
    for s in range(SLOTS):
        step(s, s < count)


def inverse_factor(matrix):
    n = matrix.shape[0]
    width = 2 * n
    at_row = lax.broadcasted_iota(jnp.int32, (n, n), 0)
    at_col = lax.broadcasted_iota(jnp.int32, (n, n), 1)
    eye = (at_row == at_col).astype(F32)
    work = jnp.concatenate([matrix, eye], axis=1)
    row_id = lax.broadcasted_iota(jnp.int32, (n, width), 0)
    for first in range(0, n, PANEL):
        columns = [
            jnp.broadcast_to(work[:, first + k : first + k + 1], (n, width)) for k in range(PANEL)
        ]
        for k in range(PANEL):
            j = first + k
            ratio = jnp.where(row_id > j, columns[k] * (1.0 / columns[k][j : j + 1]), 0.0)
            for m in range(k + 1, PANEL):
                columns[m] = columns[m] - ratio * columns[m][j : j + 1]
            work = work - ratio * work[j : j + 1]
    diag = jnp.sum(work[:, :n] * eye, axis=1, keepdims=True)
    return work[:, n:] / jnp.sqrt(diag)


def squares_kernel(ints, tiles, copies, total):
    total[...] = jnp.zeros_like(total)
    ones = jnp.ones((8, 2 * SIDE), B16)
    for s in range(0, SLOTS, 2):
        tile = tiles[s : s + 2].reshape(2 * SIDE, SIDE).astype(F32)
        sq = tile * tile
        high = sq.astype(B16)
        low = (sq - high.astype(F32)).astype(B16)
        part = dot_nt(ones, jnp.concatenate([high, low], axis=1))
        for i in range(2):
            row = part[0:1, i * SIDE : (i + 1) * SIDE]
            if s < RT_DEV:
                total[s + i : s + i + 1, :] += row
            else:
                at = pl.ds(ints[ROW + s + i], 1)
                total[at, :] += jnp.where(s + i < ints[0], row, 0.0)
    for k in range(NY):
        copies[k] = total[...]


def mass_kernel(ints, tiles, squares, start, inverse_norm, out, weights):
    inv = 1.0 / jnp.sqrt(jnp.sum(squares[...], axis=0))
    inverse_norm[...] = inv
    weights[...] = inv.astype(B16).astype(F32)
    out[...] = jnp.zeros_like(out)

    def step(s, live):
        w = jnp.broadcast_to(weights[pl.ds(ints[ROW + s], 1), :], (8, SIDE)).astype(B16)
        part = dot_nn(w, tiles[s])
        col = ints[COL + s]
        owner = col // PER_XC
        out[owner, pl.ds(col - owner * PER_XC, 1), :] += jnp.where(live, part[0:1], 0.0)

    over_slots(ints[0], step)
    v = start[...]
    gram = jnp.concatenate(
        [dot_nt(v, v, precision=highest), jnp.zeros((BLOCK, SIDE - BLOCK), F32)], axis=1
    )
    for k in range(NXC):
        out[k, PER_XC : PER_XC + 4] = gram[4 * k : 4 * k + 4]


def split_three(value):
    high = value.astype(B16)
    rest = value - high.astype(F32)
    middle = rest.astype(B16)
    return [high, middle, (rest - middle.astype(F32)).astype(B16)]


def mass_partial_kernel(parts, out):
    total = jnp.sum(parts[...], axis=0)
    gram = jnp.concatenate([total[PER_XC:], jnp.zeros((4, SIDE), F32)], axis=0)
    packed = jnp.concatenate([part.astype(F32)[0:4] for part in split_three(gram)], axis=0)
    packed = jnp.concatenate([total[0:PER_XC], packed], axis=0).astype(B16)
    for j in range(NZ):
        out[j] = packed


def mass_total_kernel(parts, out):
    total = jnp.sum(parts[...].astype(F32), axis=0)
    gram = total[PER_XC : PER_XC + 4] + total[PER_XC + 4 : PER_XC + 8] + total[PER_XC + 8 :]
    gram = jnp.concatenate([gram, jnp.zeros((4, SIDE), F32)], axis=0)
    packed = jnp.concatenate([part.astype(F32)[0:4] for part in split_three(gram)], axis=0)
    packed = jnp.concatenate([total[0:PER_XC], packed], axis=0).astype(B16)
    for k in range(NXC):
        out[k] = packed


def degree_kernel(ints, tiles, packed, start, copies, basis, total, mass):
    total[...] = jnp.zeros_like(total)
    for k in range(NXC):
        mass[k] = packed[k].astype(F32)

    def step(s, live):
        col = ints[COL + s]
        owner = col // PER_XC
        m = mass[owner, pl.ds(col - owner * PER_XC, 1), :]
        part = dot_nt(jnp.broadcast_to(m, (8, SIDE)).astype(B16), tiles[s])
        total[pl.ds(ints[ROW + s], 1), :] += jnp.where(live, part[0:1], 0.0)

    over_slots(ints[0], step)
    for k in range(NY):
        copies[k] = total[...]
    thirds = [
        jnp.concatenate(
            [mass[k, PER_XC + 4 * i : PER_XC + 4 * i + 4, 0:BLOCK] for k in range(NXC)], axis=0
        )
        for i in range(3)
    ]
    gram = thirds[0] + thirds[1] + thirds[2]
    inverse = inverse_factor(gram * (1.0 / DOCS))
    whole = dot_nn(inverse, start[...], precision=highest)
    for r in range(RT_DEV):
        basis[r] = whole[:, r * SIDE : (r + 1) * SIDE]


def term_kernel(
    ints, tiles, degrees, inverse_norm, basis, scale, keep, send, scaled, total
):
    inv = inverse_norm[...]
    degree = inv * jnp.sum(degrees[...], axis=0)
    s_all = inv / jnp.sqrt(degree)
    scale[...] = s_all
    for r in range(RT_DEV):
        scaled[r] = (basis[r] * s_all[r : r + 1, :]).astype(B16)

    def clear(i, carry):
        total[pl.ds(i * 8, 8)] = jnp.zeros((8, BLOCK, SIDE), F32)
        return carry

    lax.fori_loop(0, CT_DEV // 8, clear, 0)

    def step(s, live):
        part = dot_nn(scaled[ints[ROW + s]], tiles[s])
        total[ints[COL + s]] += jnp.where(live, part, 0.0)

    over_slots(ints[0], step)
    mine = ints[1] * HALF
    other = HALF - mine

    def write(i, carry):
        keep[pl.ds(i * 8, 8)] = total[pl.ds(mine + i * 8, 8)].astype(B16)
        send[pl.ds(i * 8, 8)] = total[pl.ds(other + i * 8, 8)].astype(B16)
        return carry

    lax.fori_loop(0, HALF // 8, write, 0)


def pair_kernel(left, right, out):
    def step(i, carry):
        at = pl.ds(i * 8, 8)
        out[at] = (left[at].astype(F32) + right[at].astype(F32)).astype(B16)
        return carry

    lax.fori_loop(0, HALF // 8, step, 0)


def close_sum_kernel(parts, out):
    def step(i, carry):
        at = pl.ds(i * PER_Z, PER_Z)
        total = parts[0, at].astype(F32)
        for k in range(1, NEAR):
            total += parts[k, at].astype(F32)
        out[at] = total.astype(B16)
        return carry

    lax.fori_loop(0, PER_NEAR // PER_Z, step, 0)


def far_sum_kernel(parts, out):
    total = parts[0].astype(F32)
    for k in range(1, NFAR):
        total += parts[k].astype(F32)
    total = total.astype(B16)
    for k in range(NFAR):
        out[k] = total


def image_sum_kernel(parts, out):
    total = parts[0].astype(F32)
    for k in range(1, NY):
        total += parts[k].astype(F32)
    for k in range(NY):
        out[k] = total


def doc_kernel(ints, tiles, own, other, out, total):
    total[...] = jnp.zeros_like(total)
    mine = ints[1]

    def step(s, live):
        col = ints[COL + s]
        half = (col >= HALF).astype(jnp.int32)
        at = col - half * HALF
        part = dot_nt(jnp.where(half == mine, own[at], other[at]), tiles[s])
        total[ints[ROW + s]] += jnp.where(live, part, 0.0)

    over_slots(ints[0], step)
    for r in range(RT_DEV):
        out[r] = total[r].astype(out.dtype)


def image_kernel(summed, scale, basis, both, copies):
    for r in range(RT_DEV):
        block = summed[r] * scale[r : r + 1, :]
        both[0:BLOCK, r * SIDE : (r + 1) * SIDE] = block
        both[BLOCK : 2 * BLOCK, r * SIDE : (r + 1) * SIDE] = basis[r]
    grams = dot_nt(both[0:BLOCK, :], both[...], precision=highest)
    packed = jnp.concatenate([grams[0:16], grams[16:32]], axis=1)
    for k in range(NXC):
        copies[k] = packed


def gram_kernel(parts, copies):
    total = jnp.sum(parts[...], axis=0)
    for j in range(NZ):
        copies[j] = total


def last_kernel(parts, both, out):
    total = jnp.sum(parts[...], axis=0) * (1.0 / DOCS)
    grams = jnp.concatenate([total[:, 0 : 2 * BLOCK], total[:, 2 * BLOCK :]], axis=0)
    coeff = grams[:, BLOCK:]
    inverse = inverse_factor(grams[:, 0:BLOCK] - dot_nt(coeff, coeff, precision=highest))
    mix = jnp.concatenate([inverse, -dot_nn(inverse, coeff, precision=highest)], axis=1)
    out[...] = dot_nn(mix, both[...], precision=highest)


def call(kernel, ins, outs, scratch=(), scalars=0, specs=None):
    shapes = [jax.ShapeDtypeStruct(shape, kind) for shape, kind in outs]
    return pl.pallas_call(
        kernel,
        out_shape=shapes,
        in_specs=specs or [SMEM] * scalars + [VMEM] * (len(ins) - scalars),
        out_specs=[VMEM] * len(shapes),
        scratch_shapes=[s if not isinstance(s, tuple) else pltpu.VMEM(*s) for s in scratch],
        compiler_params=pltpu.CompilerParams(vmem_limit_bytes=20 * 1024 * 1024),
        name=kernel.__name__,
    )(*ins)


def swap(value, axes):
    return lax.all_to_all(value, axes, 0, 0, tiled=True)


XC = ("x", "core")
Z = ("far", "pair")
CLOSE = ("pair", "x")


def body(tiles, tile_rows, tile_cols, tile_count, start):
    tiles = tiles.reshape(SLOTS, SIDE, SIDE)
    ints = jnp.concatenate(
        [
            tile_count.reshape(1),
            lax.axis_index("core").reshape(1),
            tile_rows.reshape(SLOTS),
            tile_cols.reshape(SLOTS),
        ]
    )
    full = (RT_DEV, SIDE)
    wide = (RT_DEV, BLOCK, SIDE)

    (squares,) = call(
        squares_kernel, (ints, tiles), [((NY, *full), F32)], [(full, F32)], scalars=1
    )
    squares = swap(squares, "term")
    inverse_norm, mass = call(
        mass_kernel,
        (ints, tiles, squares, start),
        [(full, F32), ((NXC, PER_XC + 4, SIDE), F32)],
        [(full, F32)],
        scalars=1,
    )
    (mass,) = call(mass_partial_kernel, (swap(mass, XC),), [((NZ, PER_XC + 12, SIDE), B16)])
    (mass,) = call(mass_total_kernel, (swap(mass, Z),), [((NXC, PER_XC + 12, SIDE), B16)])
    mass = swap(mass, XC)
    degrees, basis = call(
        degree_kernel,
        (ints, tiles, mass, start),
        [((NY, *full), F32), (wide, F32)],
        [(full, F32), ((NXC, PER_XC + 12, SIDE), F32)],
        scalars=1,
    )
    degrees = swap(degrees, "term")
    half = (HALF, BLOCK, SIDE)
    scale, keep, send = call(
        term_kernel,
        (ints, tiles, degrees, inverse_norm, basis),
        [(full, F32), (half, B16), (half, B16)],
        [(wide, B16), ((CT_DEV, BLOCK, SIDE), F32)],
        scalars=1,
    )

    def other_core(value):
        return lax.ppermute(value, "core", [(0, 1), (1, 0)])

    def spread(value, axes, parts):
        return swap(jnp.tile(value, (parts, 1, 1)), axes)

    (terms,) = call(pair_kernel, (keep, other_core(send)), [(half, B16)])
    terms = swap(terms, CLOSE).reshape(NEAR, PER_NEAR, BLOCK, SIDE)
    (terms,) = call(close_sum_kernel, (terms,), [((PER_NEAR, BLOCK, SIDE), B16)])
    terms = swap(terms, "far").reshape(NFAR, PER_Z, BLOCK, SIDE)
    (terms,) = call(far_sum_kernel, (terms,), [((NFAR, PER_Z, BLOCK, SIDE), B16)])
    terms = swap(terms.reshape(PER_NEAR, BLOCK, SIDE), "far")
    terms = spread(terms, CLOSE, NEAR)
    (partial,) = call(
        doc_kernel,
        (ints, tiles, terms, other_core(terms)),
        [(wide, SENT)],
        [(wide, F32)],
        scalars=1,
    )
    partial = swap(partial, "term").reshape(NY, RT_DEV // NY, BLOCK, SIDE)
    (summed,) = call(image_sum_kernel, (partial,), [((NY, RT_DEV // NY, BLOCK, SIDE), F32)])
    summed = swap(summed.reshape(wide), "term")
    both, grams = call(
        image_kernel,
        (summed, scale, basis),
        [((2 * BLOCK, RT_DEV * SIDE), F32), ((NXC, 16, SIDE), F32)],
    )
    (grams,) = call(gram_kernel, (swap(grams, XC),), [((NZ, 16, SIDE), F32)])
    (next_block,) = call(last_kernel, (swap(grams, Z), both), [((BLOCK, RT_DEV * SIDE), F32)])
    return next_block


def solution(mesh):
    doc = ("far", "pair", "x", "core")
    fine = Mesh(mesh.devices.reshape(NFAR, NPAIR, NX, NC, NY), (*doc, "term"))
    in_specs = (
        P(doc, "term", None, None),
        P(doc, "term"),
        P(doc, "term"),
        P(doc, "term"),
        P(None, doc),
    )
    return jax.shard_map(body, mesh=fine, in_specs=in_specs, out_specs=P(None, doc), check_vma=False)
```

```python
import jax
import jax.numpy as jnp
from jax import lax
from jax.experimental import pallas as pl
from jax.experimental.pallas import tpu as pltpu
from jax.sharding import Mesh, PartitionSpec as P

CT_DEV = 288
RT_DEV = 16
BLOCK = 32
SLOTS = 48
SIDE = 128
NZ, NX, NC, NY = 12, 4, 2, 8
NPAIR = 2
NFAR = NZ // NPAIR
NEAR = NPAIR * NX
NXC = NX * NC
PER_XC = CT_DEV // NXC
PER_Z = PER_XC // NZ
PER_NEAR = CT_DEV // NC // NEAR
ROW = 2
COL = ROW + SLOTS
PANEL = 16
HALF = CT_DEV // NC
DOCS = RT_DEV * SIDE * NZ * NXC

F32 = jnp.float32
B16 = jnp.bfloat16
SENT = B16
highest = lax.Precision.HIGHEST

VMEM = pl.BlockSpec(memory_space=pltpu.VMEM)
SMEM = pl.BlockSpec(memory_space=pltpu.SMEM)


def dot_nn(a, b, **kw):
    return lax.dot_general(a, b, (((1,), (0,)), ((), ())), preferred_element_type=F32, **kw)


def dot_nt(a, b, **kw):
    return lax.dot_general(a, b, (((1,), (1,)), ((), ())), preferred_element_type=F32, **kw)


def over_slots(count, step):
    for s in range(SLOTS):
        step(s, s < count)


def inverse_factor(matrix):
    n = matrix.shape[0]
    width = 2 * n
    at_row = lax.broadcasted_iota(jnp.int32, (n, n), 0)
    at_col = lax.broadcasted_iota(jnp.int32, (n, n), 1)
    eye = (at_row == at_col).astype(F32)
    work = jnp.concatenate([matrix, eye], axis=1)
    row_id = lax.broadcasted_iota(jnp.int32, (n, width), 0)
    for first in range(0, n, PANEL):
        columns = [
            jnp.broadcast_to(work[:, first + k : first + k + 1], (n, width)) for k in range(PANEL)
        ]
        for k in range(PANEL):
            j = first + k
            ratio = jnp.where(row_id > j, columns[k] * (1.0 / columns[k][j : j + 1]), 0.0)
            for m in range(k + 1, PANEL):
                columns[m] = columns[m] - ratio * columns[m][j : j + 1]
            work = work - ratio * work[j : j + 1]
    diag = jnp.sum(work[:, :n] * eye, axis=1, keepdims=True)
    return work[:, n:] / jnp.sqrt(diag)


def squares_kernel(ints, tiles, copies, total):
    total[...] = jnp.zeros_like(total)
    ones = jnp.ones((8, 2 * SIDE), B16)
    for s in range(0, SLOTS, 2):
        tile = tiles[s : s + 2].reshape(2 * SIDE, SIDE).astype(F32)
        sq = tile * tile
        high = sq.astype(B16)
        low = (sq - high.astype(F32)).astype(B16)
        part = dot_nt(ones, jnp.concatenate([high, low], axis=1))
        for i in range(2):
            row = part[0:1, i * SIDE : (i + 1) * SIDE]
            if s < RT_DEV:
                total[s + i : s + i + 1, :] += row
            else:
                at = pl.ds(ints[ROW + s + i], 1)
                total[at, :] += jnp.where(s + i < ints[0], row, 0.0)
    for k in range(NY):
        copies[k] = total[...]


def split_three(value):
    high = value.astype(B16)
    rest = value - high.astype(F32)
    middle = rest.astype(B16)
    return [high, middle, (rest - middle.astype(F32)).astype(B16)]


def pack_mass(mass, gram):
    rows = jnp.concatenate([gram, jnp.zeros((7, SIDE), F32)], axis=0)
    rows = [part.astype(F32)[0:1] for part in split_three(rows)]
    return jnp.concatenate([mass, *rows, jnp.zeros((1, SIDE), F32)], axis=0).astype(B16)


def unpack_gram(total):
    return total[PER_XC : PER_XC + 1] + total[PER_XC + 1 : PER_XC + 2] + total[PER_XC + 2 : PER_XC + 3]


def mass_kernel(ints, tiles, squares, start, inverse_norm, out, weights, mass):
    inv = 1.0 / jnp.sqrt(jnp.sum(squares[...], axis=0))
    inverse_norm[...] = inv
    weights[...] = inv.astype(B16).astype(F32)
    mass[...] = jnp.zeros_like(mass)

    def step(s, live):
        w = jnp.broadcast_to(weights[pl.ds(ints[ROW + s], 1), :], (8, SIDE)).astype(B16)
        part = dot_nn(w, tiles[s])
        mass[pl.ds(ints[COL + s], 1), :] += jnp.where(live, part[0:1], 0.0)

    over_slots(ints[0], step)
    v = start[...]
    gram = dot_nt(v, v, precision=highest)
    gram = jnp.concatenate([gram[8 * q : 8 * q + 8] for q in range(4)], axis=1)
    for k in range(NXC):
        out[k] = pack_mass(mass[PER_XC * k : PER_XC * (k + 1)], gram[k : k + 1])


def mass_partial_kernel(parts, out):
    total = jnp.sum(parts[...].astype(F32), axis=0)
    packed = pack_mass(total[0:PER_XC], unpack_gram(total))
    for j in range(NZ):
        out[j] = packed


def mass_total_kernel(parts, out):
    total = jnp.sum(parts[...].astype(F32), axis=0)
    packed = pack_mass(total[0:PER_XC], unpack_gram(total))
    for k in range(NXC):
        out[k] = packed


def degree_kernel(ints, tiles, packed, start, copies, basis, total, mass):
    total[...] = jnp.zeros_like(total)
    gram = []
    for k in range(NXC):
        part = packed[k].astype(F32)
        mass[PER_XC * k : PER_XC * (k + 1)] = part[0:PER_XC]
        gram.append(unpack_gram(part))
    gram = jnp.concatenate(gram, axis=0)
    gram = jnp.concatenate([gram[:, BLOCK * q : BLOCK * (q + 1)] for q in range(4)], axis=0)

    def step(s, live):
        m = mass[pl.ds(ints[COL + s], 1), :]
        part = dot_nt(jnp.broadcast_to(m, (8, SIDE)).astype(B16), tiles[s])
        total[pl.ds(ints[ROW + s], 1), :] += jnp.where(live, part[0:1], 0.0)

    over_slots(ints[0], step)
    for k in range(NY):
        copies[k] = total[...]
    inverse = inverse_factor(gram * (1.0 / DOCS))
    whole = dot_nn(inverse, start[...], precision=highest)
    for r in range(RT_DEV):
        basis[r] = whole[:, r * SIDE : (r + 1) * SIDE]


def term_kernel(
    ints, tiles, degrees, inverse_norm, basis, scale, keep, send, scaled, total
):
    inv = inverse_norm[...]
    degree = inv * jnp.sum(degrees[...], axis=0)
    s_all = inv / jnp.sqrt(degree)
    scale[...] = s_all
    for r in range(RT_DEV):
        scaled[r] = (basis[r] * s_all[r : r + 1, :]).astype(B16)

    def clear(i, carry):
        total[pl.ds(i * 8, 8)] = jnp.zeros((8, BLOCK, SIDE), F32)
        return carry

    lax.fori_loop(0, CT_DEV // 8, clear, 0)

    def step(s, live):
        part = dot_nn(scaled[ints[ROW + s]], tiles[s])
        total[ints[COL + s]] += jnp.where(live, part, 0.0)

    over_slots(ints[0], step)
    mine = ints[1] * HALF
    other = HALF - mine

    def write(i, carry):
        keep[pl.ds(i * 8, 8)] = total[pl.ds(mine + i * 8, 8)].astype(B16)
        send[pl.ds(i * 8, 8)] = total[pl.ds(other + i * 8, 8)].astype(B16)
        return carry

    lax.fori_loop(0, HALF // 8, write, 0)


def pair_kernel(left, right, out):
    def step(i, carry):
        at = pl.ds(i * 8, 8)
        out[at] = (left[at].astype(F32) + right[at].astype(F32)).astype(B16)
        return carry

    lax.fori_loop(0, HALF // 8, step, 0)


def close_sum_kernel(parts, out):
    def step(i, carry):
        at = pl.ds(i * PER_Z, PER_Z)
        total = parts[0, at].astype(F32)
        for k in range(1, NEAR):
            total += parts[k, at].astype(F32)
        out[at] = total.astype(B16)
        return carry

    lax.fori_loop(0, PER_NEAR // PER_Z, step, 0)


def far_sum_kernel(parts, out):
    total = parts[0].astype(F32)
    for k in range(1, NFAR):
        total += parts[k].astype(F32)
    total = total.astype(B16)
    for k in range(NFAR):
        out[k] = total


def image_sum_kernel(parts, out):
    total = parts[0].astype(F32)
    for k in range(1, NY):
        total += parts[k].astype(F32)
    for k in range(NY):
        out[k] = total


def doc_kernel(ints, tiles, own, other, out, total):
    total[...] = jnp.zeros_like(total)
    mine = ints[1]

    def step(s, live):
        col = ints[COL + s]
        half = (col >= HALF).astype(jnp.int32)
        at = col - half * HALF
        part = dot_nt(jnp.where(half == mine, own[at], other[at]), tiles[s])
        total[ints[ROW + s]] += jnp.where(live, part, 0.0)

    over_slots(ints[0], step)
    for r in range(RT_DEV):
        out[r] = total[r].astype(out.dtype)


def image_kernel(summed, scale, basis, both, copies):
    for r in range(RT_DEV):
        block = summed[r] * scale[r : r + 1, :]
        both[0:BLOCK, r * SIDE : (r + 1) * SIDE] = block
        both[BLOCK : 2 * BLOCK, r * SIDE : (r + 1) * SIDE] = basis[r]
    grams = dot_nt(both[0:BLOCK, :], both[...], precision=highest)
    packed = jnp.concatenate([grams[0:16], grams[16:32]], axis=1)
    for k in range(NXC):
        copies[k] = packed


def gram_kernel(parts, copies):
    total = jnp.sum(parts[...], axis=0)
    for j in range(NZ):
        copies[j] = total


def last_kernel(parts, both, out):
    total = jnp.sum(parts[...], axis=0) * (1.0 / DOCS)
    grams = jnp.concatenate([total[:, 0 : 2 * BLOCK], total[:, 2 * BLOCK :]], axis=0)
    coeff = grams[:, BLOCK:]
    inverse = inverse_factor(grams[:, 0:BLOCK] - dot_nt(coeff, coeff, precision=highest))
    mix = jnp.concatenate([inverse, -dot_nn(inverse, coeff, precision=highest)], axis=1)
    out[...] = dot_nn(mix, both[...], precision=highest)


def call(kernel, ins, outs, scratch=(), scalars=0, specs=None):
    shapes = [jax.ShapeDtypeStruct(shape, kind) for shape, kind in outs]
    return pl.pallas_call(
        kernel,
        out_shape=shapes,
        in_specs=specs or [SMEM] * scalars + [VMEM] * (len(ins) - scalars),
        out_specs=[VMEM] * len(shapes),
        scratch_shapes=[s if not isinstance(s, tuple) else pltpu.VMEM(*s) for s in scratch],
        compiler_params=pltpu.CompilerParams(vmem_limit_bytes=20 * 1024 * 1024),
        name=kernel.__name__,
    )(*ins)


def swap(value, axes):
    return lax.all_to_all(value, axes, 0, 0, tiled=True)


XC = ("x", "core")
Z = ("far", "pair")
CLOSE = ("pair", "x")


def body(tiles, tile_rows, tile_cols, tile_count, start):
    tiles = tiles.reshape(SLOTS, SIDE, SIDE)
    ints = jnp.concatenate(
        [
            tile_count.reshape(1),
            lax.axis_index("core").reshape(1),
            tile_rows.reshape(SLOTS),
            tile_cols.reshape(SLOTS),
        ]
    )
    full = (RT_DEV, SIDE)
    wide = (RT_DEV, BLOCK, SIDE)

    (squares,) = call(
        squares_kernel, (ints, tiles), [((NY, *full), F32)], [(full, F32)], scalars=1
    )
    squares = swap(squares, "term")
    inverse_norm, mass = call(
        mass_kernel,
        (ints, tiles, squares, start),
        [(full, F32), ((NXC, PER_XC + 4, SIDE), B16)],
        [(full, F32), ((CT_DEV, SIDE), F32)],
        scalars=1,
    )
    (mass,) = call(mass_partial_kernel, (swap(mass, XC),), [((NZ, PER_XC + 4, SIDE), B16)])
    (mass,) = call(mass_total_kernel, (swap(mass, Z),), [((NXC, PER_XC + 4, SIDE), B16)])
    mass = swap(mass, XC)
    degrees, basis = call(
        degree_kernel,
        (ints, tiles, mass, start),
        [((NY, *full), F32), (wide, F32)],
        [(full, F32), ((CT_DEV, SIDE), F32)],
        scalars=1,
    )
    degrees = swap(degrees, "term")
    half = (HALF, BLOCK, SIDE)
    scale, keep, send = call(
        term_kernel,
        (ints, tiles, degrees, inverse_norm, basis),
        [(full, F32), (half, B16), (half, B16)],
        [(wide, B16), ((CT_DEV, BLOCK, SIDE), F32)],
        scalars=1,
    )

    def other_core(value):
        return lax.ppermute(value, "core", [(0, 1), (1, 0)])

    def spread(value, axes, parts):
        return swap(jnp.tile(value, (parts, 1, 1)), axes)

    (terms,) = call(pair_kernel, (keep, other_core(send)), [(half, B16)])
    terms = swap(terms, CLOSE).reshape(NEAR, PER_NEAR, BLOCK, SIDE)
    (terms,) = call(close_sum_kernel, (terms,), [((PER_NEAR, BLOCK, SIDE), B16)])
    terms = swap(terms, "far").reshape(NFAR, PER_Z, BLOCK, SIDE)
    (terms,) = call(far_sum_kernel, (terms,), [((NFAR, PER_Z, BLOCK, SIDE), B16)])
    terms = swap(terms.reshape(PER_NEAR, BLOCK, SIDE), "far")
    terms = spread(terms, CLOSE, NEAR)
    (partial,) = call(
        doc_kernel,
        (ints, tiles, terms, other_core(terms)),
        [(wide, SENT)],
        [(wide, F32)],
        scalars=1,
    )
    partial = swap(partial, "term").reshape(NY, RT_DEV // NY, BLOCK, SIDE)
    (summed,) = call(image_sum_kernel, (partial,), [((NY, RT_DEV // NY, BLOCK, SIDE), F32)])
    summed = swap(summed.reshape(wide), "term")
    both, grams = call(
        image_kernel,
        (summed, scale, basis),
        [((2 * BLOCK, RT_DEV * SIDE), F32), ((NXC, 16, SIDE), F32)],
    )
    (grams,) = call(gram_kernel, (swap(grams, XC),), [((NZ, 16, SIDE), F32)])
    (next_block,) = call(last_kernel, (swap(grams, Z), both), [((BLOCK, RT_DEV * SIDE), F32)])
    return next_block


def solution(mesh):
    doc = ("far", "pair", "x", "core")
    fine = Mesh(mesh.devices.reshape(NFAR, NPAIR, NX, NC, NY), (*doc, "term"))
    in_specs = (
        P(doc, "term", None, None),
        P(doc, "term"),
        P(doc, "term"),
        P(doc, "term"),
        P(None, doc),
    )
    return jax.shard_map(body, mesh=fine, in_specs=in_specs, out_specs=P(None, doc), check_vma=False)
```

```python
import jax
import jax.numpy as jnp
from jax import lax
from jax.experimental import pallas as pl
from jax.experimental.pallas import tpu as pltpu
from jax.sharding import Mesh, PartitionSpec as P

CT_DEV = 288
RT_DEV = 16
BLOCK = 32
SLOTS = 48
SIDE = 128
NZ, NX, NC, NY = 12, 4, 2, 8
NPAIR = 2
NFAR = NZ // NPAIR
NEAR = NPAIR * NX
NXC = NX * NC
PER_XC = CT_DEV // NXC
PER_Z = PER_XC // NZ
PER_NEAR = CT_DEV // NC // NEAR
ROW = 2
COL = ROW + SLOTS
PANEL = 16
HALF = CT_DEV // NC
DOCS = RT_DEV * SIDE * NZ * NXC

F32 = jnp.float32
B16 = jnp.bfloat16
SENT = B16
highest = lax.Precision.HIGHEST

VMEM = pl.BlockSpec(memory_space=pltpu.VMEM)
SMEM = pl.BlockSpec(memory_space=pltpu.SMEM)


def dot_nn(a, b, **kw):
    return lax.dot_general(a, b, (((1,), (0,)), ((), ())), preferred_element_type=F32, **kw)


def dot_nt(a, b, **kw):
    return lax.dot_general(a, b, (((1,), (1,)), ((), ())), preferred_element_type=F32, **kw)


def over_slots(count, step):
    for s in range(SLOTS):
        step(s, s < count)


def inverse_factor(matrix):
    n = matrix.shape[0]
    width = 2 * n
    at_row = lax.broadcasted_iota(jnp.int32, (n, n), 0)
    at_col = lax.broadcasted_iota(jnp.int32, (n, n), 1)
    eye = (at_row == at_col).astype(F32)
    work = jnp.concatenate([matrix, eye], axis=1)
    row_id = lax.broadcasted_iota(jnp.int32, (n, width), 0)
    for first in range(0, n, PANEL):
        columns = [
            jnp.broadcast_to(work[:, first + k : first + k + 1], (n, width)) for k in range(PANEL)
        ]
        for k in range(PANEL):
            j = first + k
            ratio = jnp.where(row_id > j, columns[k] * (1.0 / columns[k][j : j + 1]), 0.0)
            for m in range(k + 1, PANEL):
                columns[m] = columns[m] - ratio * columns[m][j : j + 1]
            work = work - ratio * work[j : j + 1]
    diag = jnp.sum(work[:, :n] * eye, axis=1, keepdims=True)
    return work[:, n:] / jnp.sqrt(diag)


def squares_kernel(ints, tiles, copies, total):
    total[...] = jnp.zeros_like(total)
    ones = jnp.ones((8, 2 * SIDE), B16)
    for s in range(0, SLOTS, 2):
        tile = tiles[s : s + 2].reshape(2 * SIDE, SIDE).astype(F32)
        sq = tile * tile
        high = sq.astype(B16)
        low = (sq - high.astype(F32)).astype(B16)
        part = dot_nt(ones, jnp.concatenate([high, low], axis=1))
        for i in range(2):
            row = part[0:1, i * SIDE : (i + 1) * SIDE]
            if s < RT_DEV:
                total[s + i : s + i + 1, :] += row
            else:
                at = pl.ds(ints[ROW + s + i], 1)
                total[at, :] += jnp.where(s + i < ints[0], row, 0.0)
    for k in range(NY):
        copies[k] = total[...]


def split_three(value):
    high = value.astype(B16)
    rest = value - high.astype(F32)
    middle = rest.astype(B16)
    return [high, middle, (rest - middle.astype(F32)).astype(B16)]


def pack_mass(mass, gram):
    rows = jnp.concatenate([gram, jnp.zeros((7, SIDE), F32)], axis=0)
    rows = [part.astype(F32)[0:1] for part in split_three(rows)]
    return jnp.concatenate([mass, *rows, jnp.zeros((1, SIDE), F32)], axis=0).astype(B16)


def unpack_gram(total):
    return total[PER_XC : PER_XC + 1] + total[PER_XC + 1 : PER_XC + 2] + total[PER_XC + 2 : PER_XC + 3]


def mass_kernel(ints, tiles, squares, start, inverse_norm, out, weights, mass):
    inv = 1.0 / jnp.sqrt(jnp.sum(squares[...], axis=0))
    inverse_norm[...] = inv
    weights[...] = inv.astype(B16).astype(F32)
    mass[...] = jnp.zeros_like(mass)

    def step(s, live):
        w = jnp.broadcast_to(weights[pl.ds(ints[ROW + s], 1), :], (8, SIDE)).astype(B16)
        part = dot_nn(w, tiles[s])
        mass[pl.ds(ints[COL + s], 1), :] += jnp.where(live, part[0:1], 0.0)

    over_slots(ints[0], step)
    v = start[...]
    gram = dot_nt(v, v, precision=highest)
    gram = jnp.concatenate([gram[8 * q : 8 * q + 8] for q in range(4)], axis=1)
    for k in range(NXC):
        out[k] = pack_mass(mass[PER_XC * k : PER_XC * (k + 1)], gram[k : k + 1])


def mass_partial_kernel(parts, out):
    total = jnp.sum(parts[...].astype(F32), axis=0)
    packed = pack_mass(total[0:PER_XC], unpack_gram(total))
    for j in range(NZ):
        out[j] = packed


def mass_total_kernel(parts, out):
    total = jnp.sum(parts[...].astype(F32), axis=0)
    packed = pack_mass(total[0:PER_XC], unpack_gram(total))
    for k in range(NXC):
        out[k] = packed


def degree_kernel(ints, tiles, packed, start, copies, basis, total, mass):
    total[...] = jnp.zeros_like(total)
    gram = []
    for k in range(NXC):
        part = packed[k].astype(F32)
        mass[PER_XC * k : PER_XC * (k + 1)] = part[0:PER_XC]
        gram.append(unpack_gram(part))
    gram = jnp.concatenate(gram, axis=0)
    gram = jnp.concatenate([gram[:, BLOCK * q : BLOCK * (q + 1)] for q in range(4)], axis=0)

    def step(s, live):
        m = mass[pl.ds(ints[COL + s], 1), :]
        part = dot_nt(jnp.broadcast_to(m, (8, SIDE)).astype(B16), tiles[s])
        total[pl.ds(ints[ROW + s], 1), :] += jnp.where(live, part[0:1], 0.0)

    over_slots(ints[0], step)
    for k in range(NY):
        copies[k] = total[...]
    inverse = inverse_factor(gram * (1.0 / DOCS))
    whole = dot_nn(inverse, start[...], precision=highest)
    for r in range(RT_DEV):
        basis[r] = whole[:, r * SIDE : (r + 1) * SIDE]


def half_sums(ints, tiles, scaled, half, out, total):
    def clear(i, carry):
        total[pl.ds(i * 8, 8)] = jnp.zeros((8, BLOCK, SIDE), F32)
        return carry

    lax.fori_loop(0, HALF // 8, clear, 0)
    first = half * HALF

    def step(s, live):
        at = ints[COL + s] - first
        here = jnp.logical_and(live, jnp.logical_and(at >= 0, at < HALF))
        part = dot_nn(scaled[ints[ROW + s]], tiles[s])
        total[jnp.where(here, at, 0)] += jnp.where(here, part, 0.0)

    over_slots(ints[0], step)

    def write(i, carry):
        out[pl.ds(i * 8, 8)] = total[pl.ds(i * 8, 8)].astype(B16)
        return carry

    lax.fori_loop(0, HALF // 8, write, 0)


def send_kernel(ints, tiles, degrees, inverse_norm, basis, scale, scaled, send, total):
    inv = inverse_norm[...]
    degree = inv * jnp.sum(degrees[...], axis=0)
    s_all = inv / jnp.sqrt(degree)
    scale[...] = s_all
    for r in range(RT_DEV):
        scaled[r] = (basis[r] * s_all[r : r + 1, :]).astype(B16)
    half_sums(ints, tiles, scaled, 1 - ints[1], send, total)


def keep_kernel(ints, tiles, scaled, keep, total):
    half_sums(ints, tiles, scaled, ints[1], keep, total)


def pair_kernel(left, right, out):
    def step(i, carry):
        at = pl.ds(i * 8, 8)
        out[at] = (left[at].astype(F32) + right[at].astype(F32)).astype(B16)
        return carry

    lax.fori_loop(0, HALF // 8, step, 0)


def close_sum_kernel(parts, out):
    def step(i, carry):
        at = pl.ds(i * PER_Z, PER_Z)
        total = parts[0, at].astype(F32)
        for k in range(1, NEAR):
            total += parts[k, at].astype(F32)
        out[at] = total.astype(B16)
        return carry

    lax.fori_loop(0, PER_NEAR // PER_Z, step, 0)


def far_sum_kernel(parts, out):
    total = parts[0].astype(F32)
    for k in range(1, NFAR):
        total += parts[k].astype(F32)
    total = total.astype(B16)
    for k in range(NFAR):
        out[k] = total


def image_sum_kernel(parts, out):
    total = parts[0].astype(F32)
    for k in range(1, NY):
        total += parts[k].astype(F32)
    for k in range(NY):
        out[k] = total


def doc_kernel(ints, tiles, own, other, out, total):
    total[...] = jnp.zeros_like(total)
    mine = ints[1]

    def step(s, live):
        col = ints[COL + s]
        half = (col >= HALF).astype(jnp.int32)
        at = col - half * HALF
        part = dot_nt(jnp.where(half == mine, own[at], other[at]), tiles[s])
        total[ints[ROW + s]] += jnp.where(live, part, 0.0)

    over_slots(ints[0], step)
    for r in range(RT_DEV):
        out[r] = total[r].astype(out.dtype)


def image_kernel(summed, scale, basis, both, copies):
    for r in range(RT_DEV):
        block = summed[r] * scale[r : r + 1, :]
        both[0:BLOCK, r * SIDE : (r + 1) * SIDE] = block
        both[BLOCK : 2 * BLOCK, r * SIDE : (r + 1) * SIDE] = basis[r]
    grams = dot_nt(both[0:BLOCK, :], both[...], precision=highest)
    packed = jnp.concatenate([grams[0:16], grams[16:32]], axis=1)
    for k in range(NXC):
        copies[k] = packed


def gram_kernel(parts, copies):
    total = jnp.sum(parts[...], axis=0)
    for j in range(NZ):
        copies[j] = total


def last_kernel(parts, both, out):
    total = jnp.sum(parts[...], axis=0) * (1.0 / DOCS)
    grams = jnp.concatenate([total[:, 0 : 2 * BLOCK], total[:, 2 * BLOCK :]], axis=0)
    coeff = grams[:, BLOCK:]
    inverse = inverse_factor(grams[:, 0:BLOCK] - dot_nt(coeff, coeff, precision=highest))
    residual = both[0:BLOCK, :] - dot_nn(coeff, both[BLOCK:, :], precision=highest)
    out[...] = dot_nn(inverse, residual, precision=highest)


def call(kernel, ins, outs, scratch=(), scalars=0, specs=None):
    shapes = [jax.ShapeDtypeStruct(shape, kind) for shape, kind in outs]
    return pl.pallas_call(
        kernel,
        out_shape=shapes,
        in_specs=specs or [SMEM] * scalars + [VMEM] * (len(ins) - scalars),
        out_specs=[VMEM] * len(shapes),
        scratch_shapes=[s if not isinstance(s, tuple) else pltpu.VMEM(*s) for s in scratch],
        compiler_params=pltpu.CompilerParams(vmem_limit_bytes=20 * 1024 * 1024),
        name=kernel.__name__,
    )(*ins)


def swap(value, axes):
    return lax.all_to_all(value, axes, 0, 0, tiled=True)


XC = ("x", "core")
Z = ("far", "pair")
CLOSE = ("pair", "x")


def body(tiles, tile_rows, tile_cols, tile_count, start):
    tiles = tiles.reshape(SLOTS, SIDE, SIDE)
    ints = jnp.concatenate(
        [
            tile_count.reshape(1),
            lax.axis_index("core").reshape(1),
            tile_rows.reshape(SLOTS),
            tile_cols.reshape(SLOTS),
        ]
    )
    full = (RT_DEV, SIDE)
    wide = (RT_DEV, BLOCK, SIDE)

    (squares,) = call(
        squares_kernel, (ints, tiles), [((NY, *full), F32)], [(full, F32)], scalars=1
    )
    squares = swap(squares, "term")
    inverse_norm, mass = call(
        mass_kernel,
        (ints, tiles, squares, start),
        [(full, F32), ((NXC, PER_XC + 4, SIDE), B16)],
        [(full, F32), ((CT_DEV, SIDE), F32)],
        scalars=1,
    )
    (mass,) = call(mass_partial_kernel, (swap(mass, XC),), [((NZ, PER_XC + 4, SIDE), B16)])
    (mass,) = call(mass_total_kernel, (swap(mass, Z),), [((NXC, PER_XC + 4, SIDE), B16)])
    mass = swap(mass, XC)
    degrees, basis = call(
        degree_kernel,
        (ints, tiles, mass, start),
        [((NY, *full), F32), (wide, F32)],
        [(full, F32), ((CT_DEV, SIDE), F32)],
        scalars=1,
    )
    degrees = swap(degrees, "term")
    half = (HALF, BLOCK, SIDE)
    scale, scaled, send = call(
        send_kernel,
        (ints, tiles, degrees, inverse_norm, basis),
        [(full, F32), (wide, B16), (half, B16)],
        [(half, F32)],
        scalars=1,
    )
    (keep,) = call(keep_kernel, (ints, tiles, scaled), [(half, B16)], [(half, F32)], scalars=1)

    def other_core(value):
        return lax.ppermute(value, "core", [(0, 1), (1, 0)])

    def spread(value, axes, parts):
        return swap(jnp.tile(value, (parts, 1, 1)), axes)

    (terms,) = call(pair_kernel, (keep, other_core(send)), [(half, B16)])
    terms = swap(terms, CLOSE).reshape(NEAR, PER_NEAR, BLOCK, SIDE)
    (terms,) = call(close_sum_kernel, (terms,), [((PER_NEAR, BLOCK, SIDE), B16)])
    terms = swap(terms, "far").reshape(NFAR, PER_Z, BLOCK, SIDE)
    (terms,) = call(far_sum_kernel, (terms,), [((NFAR, PER_Z, BLOCK, SIDE), B16)])
    terms = swap(terms.reshape(PER_NEAR, BLOCK, SIDE), "far")
    terms = spread(terms, CLOSE, NEAR)
    (partial,) = call(
        doc_kernel,
        (ints, tiles, terms, other_core(terms)),
        [(wide, SENT)],
        [(wide, F32)],
        scalars=1,
    )
    partial = swap(partial, "term").reshape(NY, RT_DEV // NY, BLOCK, SIDE)
    (summed,) = call(image_sum_kernel, (partial,), [((NY, RT_DEV // NY, BLOCK, SIDE), F32)])
    summed = swap(summed.reshape(wide), "term")
    both, grams = call(
        image_kernel,
        (summed, scale, basis),
        [((2 * BLOCK, RT_DEV * SIDE), F32), ((NXC, 16, SIDE), F32)],
    )
    (grams,) = call(gram_kernel, (swap(grams, XC),), [((NZ, 16, SIDE), F32)])
    (next_block,) = call(last_kernel, (swap(grams, Z), both), [((BLOCK, RT_DEV * SIDE), F32)])
    return next_block


def solution(mesh):
    doc = ("far", "pair", "x", "core")
    fine = Mesh(mesh.devices.reshape(NFAR, NPAIR, NX, NC, NY), (*doc, "term"))
    in_specs = (
        P(doc, "term", None, None),
        P(doc, "term"),
        P(doc, "term"),
        P(doc, "term"),
        P(None, doc),
    )
    return jax.shard_map(body, mesh=fine, in_specs=in_specs, out_specs=P(None, doc), check_vma=False)
```

```python
import jax
import jax.numpy as jnp
from jax import lax
from jax.experimental import pallas as pl
from jax.experimental.pallas import tpu as pltpu
from jax.sharding import Mesh, PartitionSpec as P

CT_DEV = 288
RT_DEV = 16
BLOCK = 32
SLOTS = 48
SIDE = 128
NZ, NX, NC, NY = 12, 4, 2, 8
NPAIR = 2
NFAR = NZ // NPAIR
NEAR = NPAIR * NX
NXC = NX * NC
PER_XC = CT_DEV // NXC
PER_Z = PER_XC // NZ
PER_NEAR = CT_DEV // NC // NEAR
ROW = 2
COL = ROW + SLOTS
PANEL = 16
HALF = CT_DEV // NC
DOCS = RT_DEV * SIDE * NZ * NXC

F32 = jnp.float32
B16 = jnp.bfloat16
SENT = B16
highest = lax.Precision.HIGHEST

VMEM = pl.BlockSpec(memory_space=pltpu.VMEM)
SMEM = pl.BlockSpec(memory_space=pltpu.SMEM)


def dot_nn(a, b, **kw):
    return lax.dot_general(a, b, (((1,), (0,)), ((), ())), preferred_element_type=F32, **kw)


def dot_nt(a, b, **kw):
    return lax.dot_general(a, b, (((1,), (1,)), ((), ())), preferred_element_type=F32, **kw)


def over_slots(count, step):
    for s in range(SLOTS):
        step(s, s < count)


def inverse_factor(matrix):
    n = matrix.shape[0]
    width = 2 * n
    at_row = lax.broadcasted_iota(jnp.int32, (n, n), 0)
    at_col = lax.broadcasted_iota(jnp.int32, (n, n), 1)
    eye = (at_row == at_col).astype(F32)
    work = jnp.concatenate([matrix, eye], axis=1)
    row_id = lax.broadcasted_iota(jnp.int32, (n, width), 0)
    for first in range(0, n, PANEL):
        columns = [
            jnp.broadcast_to(work[:, first + k : first + k + 1], (n, width)) for k in range(PANEL)
        ]
        for k in range(PANEL):
            j = first + k
            ratio = jnp.where(row_id > j, columns[k] * (1.0 / columns[k][j : j + 1]), 0.0)
            for m in range(k + 1, PANEL):
                columns[m] = columns[m] - ratio * columns[m][j : j + 1]
            work = work - ratio * work[j : j + 1]
    diag = jnp.sum(work[:, :n] * eye, axis=1, keepdims=True)
    return work[:, n:] / jnp.sqrt(diag)


def squares_kernel(ints, tiles, copies, total):
    total[...] = jnp.zeros_like(total)
    ones = jnp.ones((8, 2 * SIDE), B16)
    for s in range(0, SLOTS, 2):
        tile = tiles[s : s + 2].reshape(2 * SIDE, SIDE).astype(F32)
        sq = tile * tile
        high = sq.astype(B16)
        low = (sq - high.astype(F32)).astype(B16)
        part = dot_nt(ones, jnp.concatenate([high, low], axis=1))
        for i in range(2):
            row = part[0:1, i * SIDE : (i + 1) * SIDE]
            if s < RT_DEV:
                total[s + i : s + i + 1, :] += row
            else:
                at = pl.ds(ints[ROW + s + i], 1)
                total[at, :] += jnp.where(s + i < ints[0], row, 0.0)
    for k in range(NY):
        copies[k] = total[...]


def split_three(value):
    high = value.astype(B16)
    rest = value - high.astype(F32)
    middle = rest.astype(B16)
    return [high, middle, (rest - middle.astype(F32)).astype(B16)]


def pack_mass(mass, gram):
    rows = jnp.concatenate([gram, jnp.zeros((7, SIDE), F32)], axis=0)
    rows = [part.astype(F32)[0:1] for part in split_three(rows)]
    return jnp.concatenate([mass, *rows, jnp.zeros((1, SIDE), F32)], axis=0).astype(B16)


def unpack_gram(total):
    return total[PER_XC : PER_XC + 1] + total[PER_XC + 1 : PER_XC + 2] + total[PER_XC + 2 : PER_XC + 3]


def mass_kernel(ints, tiles, squares, start, inverse_norm, out, weights, mass):
    inv = 1.0 / jnp.sqrt(jnp.sum(squares[...], axis=0))
    inverse_norm[...] = inv
    weights[...] = inv.astype(B16).astype(F32)
    mass[...] = jnp.zeros_like(mass)

    def step(s, live):
        w = jnp.broadcast_to(weights[pl.ds(ints[ROW + s], 1), :], (8, SIDE)).astype(B16)
        part = dot_nn(w, tiles[s])
        mass[pl.ds(ints[COL + s], 1), :] += jnp.where(live, part[0:1], 0.0)

    over_slots(ints[0], step)
    v = start[...]
    gram = dot_nt(v, v, precision=highest)
    gram = jnp.concatenate([gram[8 * q : 8 * q + 8] for q in range(4)], axis=1)
    for k in range(NXC):
        out[k] = pack_mass(mass[PER_XC * k : PER_XC * (k + 1)], gram[k : k + 1])


def mass_partial_kernel(parts, out):
    total = jnp.sum(parts[...].astype(F32), axis=0)
    packed = pack_mass(total[0:PER_XC], unpack_gram(total))
    for j in range(NZ):
        out[j] = packed


def mass_total_kernel(parts, out):
    total = jnp.sum(parts[...].astype(F32), axis=0)
    packed = pack_mass(total[0:PER_XC], unpack_gram(total))
    for k in range(NXC):
        out[k] = packed


def degree_kernel(ints, tiles, packed, start, copies, basis, total, mass):
    total[...] = jnp.zeros_like(total)
    gram = []
    for k in range(NXC):
        part = packed[k].astype(F32)
        mass[PER_XC * k : PER_XC * (k + 1)] = part[0:PER_XC]
        gram.append(unpack_gram(part))
    gram = jnp.concatenate(gram, axis=0)
    gram = jnp.concatenate([gram[:, BLOCK * q : BLOCK * (q + 1)] for q in range(4)], axis=0)

    def step(s, live):
        m = mass[pl.ds(ints[COL + s], 1), :]
        part = dot_nt(jnp.broadcast_to(m, (8, SIDE)).astype(B16), tiles[s])
        total[pl.ds(ints[ROW + s], 1), :] += jnp.where(live, part[0:1], 0.0)

    over_slots(ints[0], step)
    for k in range(NY):
        copies[k] = total[...]
    inverse = inverse_factor(gram * (1.0 / DOCS))
    whole = dot_nn(inverse, start[...], precision=highest)
    for r in range(RT_DEV):
        basis[r] = whole[:, r * SIDE : (r + 1) * SIDE]


def half_sums(ints, tiles, scaled, half, out, total):
    def clear(i, carry):
        total[pl.ds(i * 8, 8)] = jnp.zeros((8, BLOCK, SIDE), F32)
        return carry

    lax.fori_loop(0, HALF // 8, clear, 0)
    first = half * HALF

    def step(s, live):
        at = ints[COL + s] - first
        here = jnp.logical_and(live, jnp.logical_and(at >= 0, at < HALF))
        part = dot_nn(scaled[ints[ROW + s]], tiles[s])
        total[jnp.where(here, at, 0)] += jnp.where(here, part, 0.0)

    over_slots(ints[0], step)

    def write(i, carry):
        out[pl.ds(i * 8, 8)] = total[pl.ds(i * 8, 8)].astype(B16)
        return carry

    lax.fori_loop(0, HALF // 8, write, 0)


def send_kernel(ints, tiles, degrees, inverse_norm, basis, scale, scaled, send, total):
    inv = inverse_norm[...]
    degree = inv * jnp.sum(degrees[...], axis=0)
    s_all = inv / jnp.sqrt(degree)
    scale[...] = s_all
    for r in range(RT_DEV):
        scaled[r] = (basis[r] * s_all[r : r + 1, :]).astype(B16)
    half_sums(ints, tiles, scaled, 1 - ints[1], send, total)


def keep_kernel(ints, tiles, scaled, keep, total):
    half_sums(ints, tiles, scaled, ints[1], keep, total)


def pair_kernel(left, right, out):
    def step(i, carry):
        at = pl.ds(i * 8, 8)
        out[at] = (left[at].astype(F32) + right[at].astype(F32)).astype(B16)
        return carry

    lax.fori_loop(0, HALF // 8, step, 0)


def close_sum_kernel(parts, out):
    def step(i, carry):
        at = pl.ds(i * PER_Z, PER_Z)
        total = parts[0, at].astype(F32)
        for k in range(1, NEAR):
            total += parts[k, at].astype(F32)
        out[at] = total.astype(B16)
        return carry

    lax.fori_loop(0, PER_NEAR // PER_Z, step, 0)


def far_sum_kernel(parts, out):
    total = parts[0].astype(F32)
    for k in range(1, NFAR):
        total += parts[k].astype(F32)
    total = total.astype(B16)
    for k in range(NFAR):
        out[k] = total


def image_sum_kernel(parts, out):
    total = parts[0].astype(F32)
    for k in range(1, NY):
        total += parts[k].astype(F32)
    for k in range(NY):
        out[k] = total


def doc_kernel(ints, tiles, own, other, out, total):
    total[...] = jnp.zeros_like(total)
    mine = ints[1]

    def step(s, live):
        col = ints[COL + s]
        half = (col >= HALF).astype(jnp.int32)
        at = col - half * HALF
        part = dot_nt(jnp.where(half == mine, own[at], other[at]), tiles[s])
        total[ints[ROW + s]] += jnp.where(live, part, 0.0)

    over_slots(ints[0], step)
    for r in range(RT_DEV):
        out[r] = total[r].astype(out.dtype)


def image_kernel(summed, scale, basis, both, copies):
    for r in range(RT_DEV):
        block = summed[r] * scale[r : r + 1, :]
        both[0:BLOCK, r * SIDE : (r + 1) * SIDE] = block
        both[BLOCK : 2 * BLOCK, r * SIDE : (r + 1) * SIDE] = basis[r]
    grams = dot_nt(both[0:BLOCK, :], both[...], precision=highest)
    packed = jnp.concatenate([grams[0:16], grams[16:32]], axis=1)
    for k in range(NPAIR * NXC):
        copies[k] = packed


def gram_kernel(parts, copies):
    total = jnp.sum(parts[...], axis=0)
    for j in range(NFAR):
        copies[j] = total


def last_kernel(parts, both, out):
    total = jnp.sum(parts[...], axis=0) * (1.0 / DOCS)
    grams = jnp.concatenate([total[:, 0 : 2 * BLOCK], total[:, 2 * BLOCK :]], axis=0)
    coeff = grams[:, BLOCK:]
    inverse = inverse_factor(grams[:, 0:BLOCK] - dot_nt(coeff, coeff, precision=highest))
    residual = both[0:BLOCK, :] - dot_nn(coeff, both[BLOCK:, :], precision=highest)
    out[...] = dot_nn(inverse, residual, precision=highest)


def call(kernel, ins, outs, scratch=(), scalars=0, specs=None):
    shapes = [jax.ShapeDtypeStruct(shape, kind) for shape, kind in outs]
    return pl.pallas_call(
        kernel,
        out_shape=shapes,
        in_specs=specs or [SMEM] * scalars + [VMEM] * (len(ins) - scalars),
        out_specs=[VMEM] * len(shapes),
        scratch_shapes=[s if not isinstance(s, tuple) else pltpu.VMEM(*s) for s in scratch],
        compiler_params=pltpu.CompilerParams(vmem_limit_bytes=20 * 1024 * 1024),
        name=kernel.__name__,
    )(*ins)


def swap(value, axes):
    return lax.all_to_all(value, axes, 0, 0, tiled=True)


XC = ("x", "core")
Z = ("far", "pair")
CLOSE = ("pair", "x")


def body(tiles, tile_rows, tile_cols, tile_count, start):
    tiles = tiles.reshape(SLOTS, SIDE, SIDE)
    ints = jnp.concatenate(
        [
            tile_count.reshape(1),
            lax.axis_index("core").reshape(1),
            tile_rows.reshape(SLOTS),
            tile_cols.reshape(SLOTS),
        ]
    )
    full = (RT_DEV, SIDE)
    wide = (RT_DEV, BLOCK, SIDE)

    (squares,) = call(
        squares_kernel, (ints, tiles), [((NY, *full), F32)], [(full, F32)], scalars=1
    )
    squares = swap(squares, "term")
    inverse_norm, mass = call(
        mass_kernel,
        (ints, tiles, squares, start),
        [(full, F32), ((NXC, PER_XC + 4, SIDE), B16)],
        [(full, F32), ((CT_DEV, SIDE), F32)],
        scalars=1,
    )
    (mass,) = call(mass_partial_kernel, (swap(mass, XC),), [((NZ, PER_XC + 4, SIDE), B16)])
    (mass,) = call(mass_total_kernel, (swap(mass, Z),), [((NXC, PER_XC + 4, SIDE), B16)])
    mass = swap(mass, XC)
    degrees, basis = call(
        degree_kernel,
        (ints, tiles, mass, start),
        [((NY, *full), F32), (wide, F32)],
        [(full, F32), ((CT_DEV, SIDE), F32)],
        scalars=1,
    )
    degrees = swap(degrees, "term")
    half = (HALF, BLOCK, SIDE)
    scale, scaled, send = call(
        send_kernel,
        (ints, tiles, degrees, inverse_norm, basis),
        [(full, F32), (wide, B16), (half, B16)],
        [(half, F32)],
        scalars=1,
    )
    (keep,) = call(keep_kernel, (ints, tiles, scaled), [(half, B16)], [(half, F32)], scalars=1)

    def other_core(value):
        return lax.ppermute(value, "core", [(0, 1), (1, 0)])

    def spread(value, axes, parts):
        return swap(jnp.tile(value, (parts, 1, 1)), axes)

    (terms,) = call(pair_kernel, (keep, other_core(send)), [(half, B16)])
    terms = swap(terms, CLOSE).reshape(NEAR, PER_NEAR, BLOCK, SIDE)
    (terms,) = call(close_sum_kernel, (terms,), [((PER_NEAR, BLOCK, SIDE), B16)])
    terms = swap(terms, "far").reshape(NFAR, PER_Z, BLOCK, SIDE)
    (terms,) = call(far_sum_kernel, (terms,), [((NFAR, PER_Z, BLOCK, SIDE), B16)])
    terms = swap(terms.reshape(PER_NEAR, BLOCK, SIDE), "far")
    terms = spread(terms, CLOSE, NEAR)
    (partial,) = call(
        doc_kernel,
        (ints, tiles, terms, other_core(terms)),
        [(wide, SENT)],
        [(wide, F32)],
        scalars=1,
    )
    partial = swap(partial, "term").reshape(NY, RT_DEV // NY, BLOCK, SIDE)
    (summed,) = call(image_sum_kernel, (partial,), [((NY, RT_DEV // NY, BLOCK, SIDE), F32)])
    summed = swap(summed.reshape(wide), "term")
    both, grams = call(
        image_kernel,
        (summed, scale, basis),
        [((2 * BLOCK, RT_DEV * SIDE), F32), ((NPAIR * NXC, 16, SIDE), F32)],
    )
    (grams,) = call(gram_kernel, (swap(grams, ("pair", *XC)),), [((NFAR, 16, SIDE), F32)])
    (next_block,) = call(last_kernel, (swap(grams, "far"), both), [((BLOCK, RT_DEV * SIDE), F32)])
    return next_block


def solution(mesh):
    doc = ("far", "pair", "x", "core")
    fine = Mesh(mesh.devices.reshape(NFAR, NPAIR, NX, NC, NY), (*doc, "term"))
    in_specs = (
        P(doc, "term", None, None),
        P(doc, "term"),
        P(doc, "term"),
        P(doc, "term"),
        P(None, doc),
    )
    return jax.shard_map(body, mesh=fine, in_specs=in_specs, out_specs=P(None, doc), check_vma=False)
```
